256 devices in a mesh: blk: 8 (over y, core), head: 8 (over z_hi, x), dp: 4 (over z_lo).
Axes of the slice: x: 4, y: 4, z: 8 (z_hi: 2, z_lo: 4; z = z_hi * 4 + z_lo), core: 2. Of those that a mesh axis runs over, the one named last changes fastest.
Arguments:
- queries: bfloat16 [16384, 2048], P(('dp', 'blk', 'head')), parts along dimension 0, may hold values from -10 to 10
- keys: bfloat16 [16384, 2048], P(('dp', 'blk', 'head')), parts along dimension 0, may hold values from -10 to 10
- values: bfloat16 [16384, 2048], P(('dp', 'blk', 'head')), parts along dimension 0, may hold values from -6 to 6
- outputs: bfloat16 [16384, 2048], P(('dp', 'blk', 'head')), parts along dimension 0, may hold values from -6 to 6
- d_outputs: bfloat16 [16384, 2048], P(('dp', 'blk', 'head')), parts along dimension 0, may hold values from -96 to 96
- tile_mask: int32 [32, 32], replicated, may hold values from 0 to 1, as said below
- tile_order: int32 [32], replicated, may hold values from 0 to 31, each once
Outputs:
- d_queries: bfloat16 [16384, 2048], P(('dp', 'blk', 'head')), parts along dimension 0
- d_keys: bfloat16 [16384, 2048], P(('dp', 'blk', 'head')), parts along dimension 0
- d_values: bfloat16 [16384, 2048], P(('dp', 'blk', 'head')), parts along dimension 0
The draws below stay inside these ranges and needn't reach their ends.
There are 4 independent parts, one for each index of `dp`. The reference program is written for one: setup_inputs(seed, part) draws one part's arguments, and reference() takes and returns one part's arrays. A program takes and returns all parts, laid end to end along the dimension named above; an argument that names none is the same for every part. Nothing has to cross between parts.
Inputs may be any that keep to these rules, and one draw needn't show every extreme that they name: tile_mask[a, b] is 0 or 1, and 1 only where tile b lies in the window of min(3, n) tiles along each grid dimension of n tiles around tile a, shifted to stay inside; tiles are numbered with time slowest over a 2 x 4 x 4 grid; every diagonal entry is 1; in some row the whole window is 1.
All inputs are finite; a program needn't handle non-finite values.
Results may differ from the reference program's by a relative error of at most 0.005.
Values may be sent and summed in bfloat16 or wider, within the bound.
A program may use at most 64 MiB of HBM per device.

```python
import math
import jax
import jax.numpy as jnp
from jax import lax

H = 16
DH = 128
BLOCK = 128
TY = 4
TZ = 4
S = 4096
NT = 32
TX = 2


def draw_queries(key, part):
    key = jax.random.fold_in(key, 1)
    return jnp.clip(jax.random.normal(key, (S, H * DH), jnp.float32), -6.0, 6.0).astype(jnp.bfloat16)


def draw_keys(key, part):
    key = jax.random.fold_in(key, 2)
    return jnp.clip(jax.random.normal(key, (S, H * DH), jnp.float32), -6.0, 6.0).astype(jnp.bfloat16)


def draw_tile_mask(key, part):
    key = jax.random.fold_in(key, 5)
    tile_count = NT
    index_all = jnp.arange(tile_count)
    coord_x = index_all // (TY * TZ)
    coord_y = index_all // TZ % TY
    coord_z = index_all % TZ
    inside = jnp.ones((tile_count, tile_count), dtype=bool)
    for coord, extent in ((coord_x, TX), (coord_y, TY), (coord_z, TZ)):
        window = min(3, extent)
        begin = jnp.clip(coord - 1, 0, extent - window)
        inside = inside & (coord[None, :] >= begin[:, None]) & (coord[None, :] < begin[:, None] + window)
    whole_row = jax.random.randint(jax.random.fold_in(key, 1), (tile_count, 1), 0, 2) == 1
    picked = jax.random.randint(jax.random.fold_in(key, 2), (), 0, tile_count)
    keeping = jax.random.randint(jax.random.fold_in(key, 3), (tile_count, tile_count), 0, 2) == 1
    whole_row = whole_row | (index_all[:, None] == picked)
    diagonal = index_all[:, None] == index_all[None, :]
    return (inside & (keeping | whole_row | diagonal)).astype(jnp.int32)


def level_of(key, shape, cuts, smallest, high):
    def one(axis_at, parts):
        steps = jax.random.uniform(jax.random.fold_in(jax.random.fold_in(key, 6), axis_at), (parts,), jnp.float32, smallest / len(cuts), high / len(cuts))
        return jnp.repeat(jnp.exp(steps), shape[axis_at] // parts).reshape((-1,) + (1,) * (len(shape) - axis_at - 1))

    factor_of = one(*cuts[0])
    for cut in cuts[1:]:
        factor_of = factor_of * one(*cut)
    return factor_of


def normal_values(rng, dims, width, limit, pieces=(), kind=jnp.bfloat16):
    values = width * jax.random.normal(rng, dims, jnp.float32)
    if pieces:
        values = values * level_of(rng, dims, pieces, -0.22, 0.18)
    return jnp.clip(values, -limit, limit).astype(kind)


def setup_inputs(seed: int = 0, part: int = 0) -> dict:
    key_of = jax.random.split(jax.random.key(seed), 8)
    part_splits = jax.random.split(jax.random.fold_in(key_of[7], part), 8)
    return {
        "queries": draw_queries(jax.random.fold_in(jax.random.fold_in(key_of[7], part), 71), part),
        "keys": draw_keys(jax.random.fold_in(jax.random.fold_in(key_of[7], part), 71), part),
        "values": normal_values(part_splits[2], (S, H * DH), 1.0, 6.0, ((0, 64),)),
        "outputs": normal_values(part_splits[3], (S, H * DH), 1.0, 6.0, ((0, 64),)),
        "d_outputs": normal_values(part_splits[4], (S, H * DH), 16.0, 96.0, ((0, 64),)),
        "tile_mask": draw_tile_mask(jax.random.fold_in(key_of[7], 71), part),
        "tile_order": jax.random.permutation(key_of[6], NT).astype(jnp.int32),
    }


def head_grads(arrays, allowed_blocks):
    query_head, key_head, value_head, output_head, dout_head = arrays
    factor = DH ** -0.5
    block_rows = math.gcd(S, 512)
    block_count = S // block_rows
    delta_all = jnp.sum(dout_head.astype(jnp.float32) * output_head.astype(jnp.float32), axis=1)

    def advance(carried, block_index):
        key_acc, value_acc = carried
        offset = (block_index * block_rows).astype(jnp.int32)
        query_rows = lax.dynamic_slice_in_dim(query_head, offset, block_rows, 0)
        dout_rows = lax.dynamic_slice_in_dim(dout_head, offset, block_rows, 0)
        delta_rows = lax.dynamic_slice_in_dim(delta_all, offset, block_rows, 0)
        tile_rows = lax.dynamic_slice_in_dim(allowed_blocks, (block_index * (block_rows // BLOCK)).astype(jnp.int32), block_rows // BLOCK, 0)
        allowed = jnp.repeat(jnp.repeat(tile_rows, BLOCK, axis=0), BLOCK, axis=1)
        scores = jnp.dot(query_rows, key_head.T, preferred_element_type=jnp.float32) * factor
        masked = jnp.where(allowed, scores, -1.0e30)
        row_top = jnp.max(masked, axis=1, keepdims=True)
        log_total = row_top + jnp.log(jnp.sum(jnp.where(allowed, jnp.exp(masked - row_top), 0.0), axis=1, keepdims=True))
        probs = jnp.where(allowed, jnp.exp(scores - log_total), 0.0)
        dprobs = jnp.dot(dout_rows, value_head.T, preferred_element_type=jnp.float32)
        dscores = (factor * probs * (dprobs - delta_rows[:, None])).astype(jnp.bfloat16)
        probs_low = probs.astype(jnp.bfloat16)
        query_grad = jnp.dot(dscores, key_head, preferred_element_type=jnp.float32).astype(jnp.bfloat16)
        key_acc = key_acc + jnp.dot(dscores.T, query_rows, preferred_element_type=jnp.float32)
        value_acc = value_acc + jnp.dot(probs_low.T, dout_rows, preferred_element_type=jnp.float32)
        return (key_acc, value_acc), query_grad

    zeros_start = jnp.zeros((S, DH), jnp.float32)
    (key_acc, value_acc), query_blocks = lax.scan(advance, (zeros_start, zeros_start), jnp.arange(block_count, dtype=jnp.int32))
    return query_blocks.reshape(S, DH), key_acc.astype(jnp.bfloat16), value_acc.astype(jnp.bfloat16)


def reference(queries, keys, values, outputs, d_outputs, tile_mask, tile_order):
    order_index = tile_order.astype(jnp.int32)
    allowed_blocks = tile_mask[order_index][:, order_index] == 1

    def by_head(source):
        return source.reshape(S, H, DH).transpose(1, 0, 2)

    def one_head(arrays):
        return head_grads(arrays, allowed_blocks)

    stacked = (by_head(queries), by_head(keys), by_head(values), by_head(outputs), by_head(d_outputs))
    query_grads, key_grads, value_grads = lax.map(one_head, stacked)

    def merge_heads(source):
        return source.transpose(1, 0, 2).reshape(S, H * DH)

    return merge_heads(query_grads), merge_heads(key_grads), merge_heads(value_grads)
```

```python
import jax
import jax.numpy as jnp
from jax import lax
from jax.experimental import pallas as pl
from jax.experimental.pallas import tpu as pltpu
from jax.sharding import PartitionSpec as P

DH = 128
BLOCK = 128
ROWS = 64
CHIPS = 16
GROUP = 4 * ROWS
HALF = CHIPS * ROWS
CHUNK = 256
SCALE = DH**-0.5
LOG2E = 1.4426950408889634
MESH = pl.DeviceIdType.MESH
BF16 = jnp.bfloat16
F32 = jnp.float32

NT = (((1,), (1,)), ((), ()))
NN = (((1,), (0,)), ((), ()))
TN = (((0,), (0,)), ((), ()))


def mm(a, b, dims):
    return lax.dot_general(a, b, dims, preferred_element_type=F32)


def rows(start, size):
    return pl.ds(pl.multiple_of(start, size), size)


def kernel(
    q_ref, k_ref, v_ref, o_ref, g_ref, mask_ref, order_ref,
    dq_ref, dk_ref, dv_ref,
    qb, kb, vb, gb, ee, dka, dva, rka, rva, dqa, dqs, dqr, oq, ok, ov,
    dcol, dsrc, drec, stm, str_, bias,
    s_in, r_in, s_z, r_z, s_c, r_c, s_d, r_d, s_st, r_st, s_dz, r_dz, s_kv, r_kv, s_out, r_out,
):
    blk = lax.axis_index("blk")
    hd = lax.axis_index("head")
    dp = lax.axis_index("dp")
    y, c = blk // 2, blk % 2
    g, x = hd // 4, hd % 4
    me = y * 4 + x

    def plane(px, py):
        return (py * 2 + c, g * 4 + px, dp)

    across = (blk, (1 - g) * 4 + x, dp)
    sibling = (y * 2 + 1 - c, hd, dp)

    def remote(src, dst, ss, rs, to):
        return pltpu.make_async_remote_copy(
            src_ref=src, dst_ref=dst, send_sem=ss, recv_sem=rs, device_id=to, device_id_type=MESH
        )

    def took(ref, sem):
        pltpu.make_async_copy(ref, ref, sem).wait()

    def peer(k):
        px, py = (x + k % 4) % 4, (y + k // 4) % 4
        return px, py, py * 4 + px

    barrier = pltpu.get_barrier_semaphore()

    def greet(k, carry):
        px, py, unused = peer(k)
        pl.semaphore_signal(barrier, inc=1, device_id=plane(px, py), device_id_type=MESH)
        return carry

    pl.semaphore_signal(barrier, inc=1, device_id=across, device_id_type=MESH)
    lax.fori_loop(1, CHIPS, greet, 0)
    pl.semaphore_signal(barrier, inc=1, device_id=sibling, device_id_type=MESH)

    dcol[...] = jnp.zeros_like(dcol)
    prod = g_ref[...].astype(F32) * o_ref[...].astype(F32)
    lane = lax.broadcasted_iota(jnp.int32, (ROWS, BLOCK), 1)
    cols = jnp.zeros((ROWS, BLOCK), F32)
    for h in range(CHIPS):
        part = jnp.sum(prod[:, h * DH : (h + 1) * DH], axis=1, keepdims=True)
        cols = jnp.where(lane == h, part, cols)
    dcol[rows((x % 2) * ROWS, ROWS), :] = cols
    turned = dcol[...].T
    for h in range(CHIPS):
        dsrc[h] = turned[h : h + 1, :]

    pl.semaphore_wait(barrier, 17)

    sources = (q_ref, k_ref, g_ref, v_ref)
    targets = (qb.at[0], kb.at[c], gb.at[0], vb.at[c])
    mine = rows(me * ROWS, ROWS)
    for a in range(4):
        here = sources[a].at[:, rows(me * DH, DH)]
        pltpu.make_async_copy(here, targets[a].at[mine], r_in.at[a, y]).start()

        def send(k, carry):
            px, py, who = peer(k)
            remote(
                sources[a].at[:, rows(who * DH, DH)], targets[a].at[mine], s_in.at[a], r_in.at[a, y], plane(px, py)
            ).start()
            return carry

        lax.fori_loop(1, CHIPS, send, 0)
        if a == 1:
            pltpu.make_async_copy(dsrc.at[me], drec.at[me], r_d).start()

            def send_delta(k, carry):
                px, py, who = peer(k)
                remote(dsrc.at[who], drec.at[me], s_d, r_d, plane(px, py)).start()
                return carry

            lax.fori_loop(1, CHIPS, send_delta, 0)

    def block_of(j, core, half):
        return ((j // 2) * 2 + core) * 4 + half * 2 + j % 2

    def bias_row(i, carry):
        key_tile = order_ref[block_of(i % 8, i // 8, g)]
        for half in range(2):
            for j in range(8):
                query_tile = order_ref[block_of(j, c, g if half == 0 else 1 - g)]
                allowed = mask_ref[query_tile, key_tile]
                value = jnp.where(allowed == 1, 0.0, -1.0e30).astype(F32)
                bias[half, i, :, j * BLOCK : (j + 1) * BLOCK] = jnp.full((1, BLOCK), value, F32)
        return carry

    lax.fori_loop(0, 16, bias_row, 0)

    dka[...] = jnp.zeros_like(dka)
    dva[...] = jnp.zeros_like(dva)

    def group(k):
        return (y + 4 - k) % 4

    def forward_z(a, buf):
        def one(k, carry):
            yy = group(k)
            part = rows(yy * GROUP, GROUP)
            took(buf.at[0, part], r_in.at[2 * a, yy])
            remote(buf.at[0, part], buf.at[1, part], s_z.at[a], r_z.at[a, yy], across).start()
            return carry

        lax.fori_loop(0, 4, one, 0)

    def forward_core(a, buf):
        def one(k, carry):
            yy = group(k)
            part = rows(yy * GROUP, GROUP)
            took(buf.at[c, part], r_in.at[2 * a + 1, yy])
            remote(buf.at[c, part], buf.at[c, part], s_c.at[a], r_c.at[a], sibling).start()
            return carry

        lax.fori_loop(0, 4, one, 0)

    chunks = 2 * HALF // CHUNK

    def key_part(i):
        return i // (HALF // CHUNK), rows(i % (HALF // CHUNK) * CHUNK, CHUNK)

    def weigh(half, yy):
        lanes = rows(yy * GROUP, GROUP)
        query = qb[half, lanes, :]

        def first(i, top):
            core, part = key_part(i)
            s = mm(kb[core, part, :], query, NT) * (SCALE * LOG2E)
            low = s[:BLOCK] + bias[half, 2 * i, :, lanes]
            high = s[BLOCK:] + bias[half, 2 * i + 1, :, lanes]
            ee[half, yy, pl.ds(pl.multiple_of(i * CHUNK, CHUNK), BLOCK), :] = low
            ee[half, yy, pl.ds(pl.multiple_of(i * CHUNK + BLOCK, BLOCK), BLOCK), :] = high
            both = jnp.maximum(low, high).reshape(BLOCK // 8, 8, GROUP)
            return jnp.maximum(top, jnp.max(both, axis=0))

        top = lax.fori_loop(0, chunks, first, jnp.full((8, GROUP), -3.0e38, F32))
        top = jnp.max(top, axis=0, keepdims=True)

        def second(i, total):
            part = rows(i * CHUNK, CHUNK)
            e = jnp.exp2(ee[half, yy, part, :] - top)
            ee[half, yy, part, :] = e
            return total + jnp.sum(e.reshape(CHUNK // 8, 8, GROUP), axis=0)

        total = lax.fori_loop(0, chunks, second, jnp.zeros((8, GROUP), F32))
        stm[3 * half : 3 * half + 1, lanes] = top
        stm[3 * half + 1 : 3 * half + 2, lanes] = jnp.sum(total, axis=0, keepdims=True)

    def gradients(half, yy):
        lanes = rows(yy * GROUP, GROUP)
        query = qb[half, lanes, :]
        dout = gb[half, lanes, :]
        there = 3 - 3 * half
        top, total = stm[3 * half : 3 * half + 1, lanes], stm[3 * half + 1 : 3 * half + 2, lanes]
        top_r, total_r = str_[there : there + 1, lanes], str_[there + 1 : there + 2, lanes]
        high = jnp.maximum(top, top_r)
        ours = jnp.exp2(top - high)
        factor = ours / (total * ours + total_r * jnp.exp2(top_r - high))
        delta = stm[2:3, lanes] if half == 0 else str_[2:3, lanes]

        def one(i, dq):
            core, part = key_part(i)
            dprobs = mm(vb[core, part, :], dout, NT)
            probs = ee[half, yy, rows(i * CHUNK, CHUNK), :] * factor
            ds = (probs * (dprobs - delta)).astype(BF16)
            dva[core, part, :] += mm(probs.astype(BF16), dout, NN)
            dka[core, part, :] += mm(ds, query, NN)
            return dq + mm(ds, kb[core, part, :], TN)

        return lax.fori_loop(0, chunks, one, jnp.zeros((GROUP, DH), F32)) * SCALE

    forward_z(0, qb)
    forward_core(0, kb)
    took(kb.at[1 - c], r_c.at[0])

    def weigh_own(k, carry):
        weigh(0, group(k))
        return carry

    lax.fori_loop(0, 4, weigh_own, 0)
    forward_z(1, gb)
    forward_core(1, vb)

    took(drec, r_d)
    for j in range(8):
        stm[2:3, j * BLOCK : (j + 1) * BLOCK] = drec[2 * j] + drec[2 * j + 1]

    def weigh_other(k, carry):
        yy = group(k)
        took(qb.at[1, rows(yy * GROUP, GROUP)], r_z.at[0, yy])
        weigh(1, yy)
        return carry

    lax.fori_loop(0, 4, weigh_other, 0)
    swap = remote(stm, str_, s_st, r_st, across)
    swap.start()
    took(vb.at[1 - c], r_c.at[1])
    swap.wait_recv()

    def own(k, carry):
        yy = group(k)
        dqa[rows(yy * GROUP, GROUP), :] = gradients(0, yy)
        return carry

    lax.fori_loop(0, 4, own, 0)

    def other(k, carry):
        yy = group(k)
        part = rows(yy * GROUP, GROUP)
        took(gb.at[1, part], r_z.at[1, yy])
        dqs[part, :] = gradients(1, yy).astype(BF16)
        remote(dqs.at[part], dqr.at[part], s_dz, r_dz.at[yy], across).start()
        return carry

    lax.fori_loop(0, 4, other, 0)

    remote(dka.at[1 - c], rka, s_kv.at[0], r_kv.at[0], sibling).start()
    remote(dva.at[1 - c], rva, s_kv.at[1], r_kv.at[1], sibling).start()

    def give(buf, out, a):
        pltpu.make_async_copy(buf.at[mine], out.at[:, rows(me * DH, DH)], r_out.at[a]).start()

        def send(k, carry):
            px, py, who = peer(k)
            remote(
                buf.at[rows(who * ROWS, ROWS)], out.at[:, rows(me * DH, DH)], s_out.at[a], r_out.at[a], plane(px, py)
            ).start()
            return carry

        lax.fori_loop(1, CHIPS, send, 0)

    took(rka, r_kv.at[0])
    ok[...] = ((dka[c] + rka[...]) * SCALE).astype(BF16)
    give(ok, dk_ref, 1)
    took(rva, r_kv.at[1])
    ov[...] = (dva[c] + rva[...]).astype(BF16)
    give(ov, dv_ref, 2)

    for k in range(4):
        yy = group(k)
        part = rows(yy * GROUP, GROUP)
        took(dqr.at[part], r_dz.at[yy])
        oq[part, :] = (dqa[part, :] + dqr[part, :].astype(F32)).astype(BF16)
        for kx in range(4):
            px = (x + kx) % 4
            piece = oq.at[rows((yy * 4 + px) * ROWS, ROWS)]
            out = dq_ref.at[:, rows(me * DH, DH)]
            if k == 0 and kx == 0:
                pltpu.make_async_copy(piece, out, r_out.at[0]).start()
            else:
                remote(piece, out, s_out.at[0], r_out.at[0], plane(px, yy)).start()

    sent = pl.ds(0, HALF - ROWS)
    for a in range(4):
        took(qb.at[0, sent], s_in.at[a])
    took(drec.at[pl.ds(0, CHIPS - 1)], s_d)
    for a in range(2):
        took(qb.at[0], s_z.at[a])
        took(qb.at[0], s_c.at[a])
        took(rka, s_kv.at[a])
    swap.wait_send()
    took(dqs, s_dz)
    for a, out in enumerate((dq_ref, dk_ref, dv_ref)):
        took(out, r_out.at[a])
        took(qb.at[0, sent], s_out.at[a])


def body(queries, keys, values, outputs, d_outputs, tile_mask, tile_order):
    half = (HALF, DH)
    dma = pltpu.SemaphoreType.DMA
    vmem = pl.BlockSpec(memory_space=pltpu.VMEM)
    smem = pl.BlockSpec(memory_space=pltpu.SMEM)
    return pl.pallas_call(
        kernel,
        out_shape=[jax.ShapeDtypeStruct(queries.shape, BF16)] * 3,
        in_specs=[vmem] * 5 + [smem] * 2,
        out_specs=[vmem] * 3,
        scratch_shapes=[
            pltpu.VMEM((2,) + half, BF16),
            pltpu.VMEM((2,) + half, BF16),
            pltpu.VMEM((2,) + half, BF16),
            pltpu.VMEM((2,) + half, BF16),
            pltpu.VMEM((2, 4, 2 * HALF, GROUP), F32),
            pltpu.VMEM((2,) + half, F32),
            pltpu.VMEM((2,) + half, F32),
            pltpu.VMEM(half, F32),
            pltpu.VMEM(half, F32),
            pltpu.VMEM(half, F32),
            pltpu.VMEM(half, BF16),
            pltpu.VMEM(half, BF16),
            pltpu.VMEM(half, BF16),
            pltpu.VMEM(half, BF16),
            pltpu.VMEM(half, BF16),
            pltpu.VMEM((BLOCK, BLOCK), F32),
            pltpu.VMEM((CHIPS, 1, BLOCK), F32),
            pltpu.VMEM((CHIPS, 1, BLOCK), F32),
            pltpu.VMEM((8, HALF), F32),
            pltpu.VMEM((8, HALF), F32),
            pltpu.VMEM((2, 16, 1, HALF), F32),
            dma((4,)), dma((4, 4)),
            dma((2,)), dma((2, 4)),
            dma((2,)), dma((2,)),
            dma, dma,
            dma, dma,
            dma, dma((4,)),
            dma((2,)), dma((2,)),
            dma((3,)), dma((3,)),
        ],
        compiler_params=pltpu.CompilerParams(
            collective_id=0, has_side_effects=True, vmem_limit_bytes=48 * 2**20
        ),
        cost_estimate=pl.CostEstimate(flops=5 * 2**30, bytes_accessed=2**21, transcendentals=2**22),
        name="attention_backward",
    )(queries, keys, values, outputs, d_outputs, tile_mask, tile_order)


def solution(mesh):
    split = P(("dp", "blk", "head"), None)
    return jax.shard_map(
        body,
        mesh=mesh,
        in_specs=(split,) * 5 + (P(), P()),
        out_specs=(split,) * 3,
        check_vma=False,
    )
```

```python
import jax
import jax.numpy as jnp
from jax import lax
from jax.experimental import pallas as pl
from jax.experimental.pallas import tpu as pltpu
from jax.sharding import PartitionSpec as P

DH = 128
BLOCK = 128
ROWS = 64
CHIPS = 16
GROUP = 4 * ROWS
HALF = CHIPS * ROWS
SCALE = DH**-0.5
LOG2E = 1.4426950408889634
MESH = pl.DeviceIdType.MESH
BF16 = jnp.bfloat16
F32 = jnp.float32

NT = (((1,), (1,)), ((), ()))
NN = (((1,), (0,)), ((), ()))
TN = (((0,), (0,)), ((), ()))


def mm(a, b, dims):
    return lax.dot_general(a, b, dims, preferred_element_type=F32)


def rows(start, size):
    return pl.ds(pl.multiple_of(start, size), size)


def kernel(
    q_ref, k_ref, v_ref, o_ref, g_ref, mask_hbm, order_hbm,
    dq_ref, dk_ref, dv_ref,
    qb, kb, vb, gb, ee, dka, dva, rka, rva, dqa, dqs, dqr, oq, ok, ov,
    ol, gl, mask_ref, order_ref, dcol, dsrc, drec, st_own, st_oth, pr_own, pr_oth, bias,
    s_ld, s_in, r_in, s_z, r_z, s_c, r_c, s_d, r_d, s_st, r_st, s_so, r_so, s_dz, r_dz, s_kv, r_kv, s_out, r_out,
):
    blk = lax.axis_index("blk")
    hd = lax.axis_index("head")
    dp = lax.axis_index("dp")
    y, c = blk // 2, blk % 2
    g, x = hd // 4, hd % 4
    me = y * 4 + x

    def plane(px, py):
        return (py * 2 + c, g * 4 + px, dp)

    across = (blk, (1 - g) * 4 + x, dp)
    sibling = (y * 2 + 1 - c, hd, dp)

    def remote(src, dst, ss, rs, to):
        return pltpu.make_async_remote_copy(
            src_ref=src, dst_ref=dst, send_sem=ss, recv_sem=rs, device_id=to, device_id_type=MESH
        )

    def took(ref, sem):
        pltpu.make_async_copy(ref, ref, sem).wait()

    def peer(k):
        px, py = (x + k % 4) % 4, (y + k // 4) % 4
        return px, py, py * 4 + px

    barrier = pltpu.get_barrier_semaphore()

    def greet(k, carry):
        px, py, unused = peer(k)
        pl.semaphore_signal(barrier, inc=1, device_id=plane(px, py), device_id_type=MESH)
        return carry

    pl.semaphore_signal(barrier, inc=1, device_id=across, device_id_type=MESH)
    lax.fori_loop(1, CHIPS, greet, 0)
    pl.semaphore_signal(barrier, inc=1, device_id=sibling, device_id_type=MESH)

    loads = [
        pltpu.make_async_copy(src, dst, s_ld.at[n])
        for n, (src, dst) in enumerate(((o_ref, ol), (g_ref, gl), (mask_hbm, mask_ref), (order_hbm, order_ref)))
    ]
    for load in loads:
        load.start()
    pl.semaphore_wait(barrier, 17)

    sources = (q_ref, k_ref, g_ref, v_ref)
    mine = rows(me * ROWS, ROWS)
    mine_kv = rows(c * HALF + me * ROWS, ROWS)
    targets = (qb.at[0, mine], kb.at[mine_kv], gb.at[0, mine], vb.at[mine_kv])
    for a in range(4):
        here = sources[a].at[:, rows(me * DH, DH)]
        pltpu.make_async_copy(here, targets[a], r_in.at[a, y]).start()

        def send(k, carry):
            px, py, who = peer(k)
            remote(
                sources[a].at[:, rows(who * DH, DH)], targets[a], s_in.at[a], r_in.at[a, y], plane(px, py)
            ).start()
            return carry

        lax.fori_loop(1, CHIPS, send, 0)

    def group(k):
        return (y + 4 - k) % 4

    def forward_z(a, buf, first, last):
        def one(k, carry):
            yy = group(k)
            part = rows(yy * GROUP, GROUP)
            took(buf.at[0, part], r_in.at[2 * a, yy])
            remote(buf.at[0, part], buf.at[1, part], s_z.at[a], r_z.at[a, yy], across).start()
            return carry

        lax.fori_loop(first, last, one, 0)

    def forward_core(a, buf):
        def one(k, carry):
            yy = group(k)
            part = rows(c * HALF + yy * GROUP, GROUP)
            took(buf.at[part], r_in.at[2 * a + 1, yy])
            remote(buf.at[part], buf.at[part], s_c.at[a], r_c.at[a], sibling).start()
            return carry

        lax.fori_loop(0, 4, one, 0)

    forward_z(0, qb, 0, 4)

    for load in loads:
        load.wait()

    dcol[...] = jnp.zeros_like(dcol)
    prod = gl[...].astype(F32) * ol[...].astype(F32)
    lane = lax.broadcasted_iota(jnp.int32, (ROWS, BLOCK), 1)
    cols = jnp.zeros((ROWS, BLOCK), F32)
    for h in range(CHIPS):
        part = jnp.sum(prod[:, h * DH : (h + 1) * DH], axis=1, keepdims=True)
        cols = jnp.where(lane == h, part, cols)
    dcol[rows((x % 2) * ROWS, ROWS), :] = cols
    turned = dcol[...].T
    for h in range(CHIPS):
        dsrc[h] = turned[h : h + 1, :]

    pltpu.make_async_copy(dsrc.at[me], drec.at[me], r_d).start()

    def send_delta(k, carry):
        px, py, who = peer(k)
        remote(dsrc.at[who], drec.at[me], s_d, r_d, plane(px, py)).start()
        return carry

    lax.fori_loop(1, CHIPS, send_delta, 0)

    def block_of(j, core, half):
        return ((j // 2) * 2 + core) * 4 + half * 2 + j % 2

    def bias_row(i, carry):
        key_tile = order_ref[block_of(i % 8, i // 8, g)]
        for half in range(2):
            for j in range(8):
                query_tile = order_ref[block_of(j, c, g if half == 0 else 1 - g)]
                allowed = mask_ref[query_tile, key_tile]
                value = jnp.where(allowed == 1, 0.0, -1.0e30).astype(F32)
                bias[half, i, :, j * BLOCK : (j + 1) * BLOCK] = jnp.full((1, BLOCK), value, F32)
        return carry

    lax.fori_loop(0, 16, bias_row, 0)
    dka[...] = jnp.zeros_like(dka)
    dva[...] = jnp.zeros_like(dva)

    def weigh(half, yy, stats):
        lanes = rows(yy * GROUP, GROUP)
        s = mm(kb[...], qb[half, lanes, :], NT) * (SCALE * LOG2E)
        top = jnp.full((8, GROUP), -3.0e38, F32)
        for i in range(16):
            part = s[i * BLOCK : (i + 1) * BLOCK] + bias[half, i, :, lanes]
            ee[half, yy, i * BLOCK : (i + 1) * BLOCK, :] = part
            top = jnp.maximum(top, jnp.max(part.reshape(BLOCK // 8, 8, GROUP), axis=0))
        top = jnp.max(top, axis=0, keepdims=True)
        e = jnp.exp2(ee[half, yy] - top)
        ee[half, yy] = e
        total = jnp.sum(e.reshape(2 * HALF // 8, 8, GROUP), axis=0)
        stats[yy, 0] = top
        stats[yy, 1] = jnp.sum(total, axis=0, keepdims=True)

    def gradients(half, yy, stats, theirs, delta):
        lanes = rows(yy * GROUP, GROUP)
        query = qb[half, lanes, :]
        dout = gb[half, lanes, :]
        top, total, top_r, total_r = stats[yy, 0], stats[yy, 1], theirs[yy, 0], theirs[yy, 1]
        high = jnp.maximum(top, top_r)
        ours = jnp.exp2(top - high)
        factor = ours / (total * ours + total_r * jnp.exp2(top_r - high))
        e = ee[half, yy]
        ds = (e * (factor * SCALE) * (mm(vb[...], dout, NT) - delta)).astype(BF16)
        dva[...] += mm((e * factor).astype(BF16), dout, NN)
        dka[...] += mm(ds, query, NN)
        return mm(ds, kb[...], TN)

    def weigh_own(k, carry):
        weigh(0, group(k), st_own)
        return carry

    def weigh_other(k, carry):
        yy = group(k)
        took(qb.at[1, rows(yy * GROUP, GROUP)], r_z.at[0, yy])
        weigh(1, yy, st_oth)
        remote(st_oth.at[yy], pr_oth.at[yy], s_so, r_so.at[yy], across).start()
        return carry

    def own(k, carry):
        yy = group(k)
        took(pr_oth.at[yy], r_so.at[yy])
        dqa[rows(yy * GROUP, GROUP), :] = gradients(0, yy, st_own, pr_oth, st_own[yy, 2])
        return carry

    def other(k, carry):
        yy = group(k)
        part = rows(yy * GROUP, GROUP)
        took(gb.at[1, part], r_z.at[1, yy])
        dqs[part, :] = gradients(1, yy, st_oth, pr_own, pr_own[yy, 2]).astype(BF16)
        remote(dqs.at[part], dqr.at[part], s_dz, r_dz.at[yy], across).start()
        return carry

    forward_core(0, kb)
    forward_z(1, gb, 0, 1)
    took(kb.at[pl.ds((1 - c) * HALF, HALF)], r_c.at[0])
    lax.fori_loop(0, 3, weigh_other, 0)
    forward_z(1, gb, 1, 2)
    forward_core(1, vb)
    lax.fori_loop(0, 4, weigh_own, 0)
    took(drec, r_d)
    for j in range(8):
        st_own[j // 2, 2, :, j % 2 * BLOCK : (j % 2 + 1) * BLOCK] = drec[2 * j] + drec[2 * j + 1]
    tell = remote(st_own, pr_own, s_st, r_st, across)
    tell.start()
    lax.fori_loop(3, 4, weigh_other, 0)
    forward_z(1, gb, 2, 4)
    took(vb.at[pl.ds((1 - c) * HALF, HALF)], r_c.at[1])
    lax.fori_loop(0, 3, own, 0)
    tell.wait_recv()
    lax.fori_loop(0, 2, other, 0)
    lax.fori_loop(3, 4, own, 0)
    lax.fori_loop(2, 4, other, 0)

    for k in range(4):
        yy = group(k)
        part = rows(yy * GROUP, GROUP)
        there = rows((1 - c) * HALF + yy * GROUP, GROUP)
        remote(dva.at[there], rva.at[part], s_kv.at[1], r_kv.at[1, yy], sibling).start()
        remote(dka.at[there], rka.at[part], s_kv.at[0], r_kv.at[0, yy], sibling).start()

    def give(k, buf, out, a):
        yy = group(k)
        for kx in range(4):
            px = (x + kx) % 4
            piece = buf.at[rows((yy * 4 + px) * ROWS, ROWS)]
            home = out.at[:, rows(me * DH, DH)]
            if k == 0 and kx == 0:
                pltpu.make_async_copy(piece, home, r_out.at[a]).start()
            else:
                remote(piece, home, s_out.at[a], r_out.at[a], plane(px, yy)).start()

    for k in range(4):
        yy = group(k)
        part = rows(yy * GROUP, GROUP)
        here = rows(c * HALF + yy * GROUP, GROUP)
        took(rva.at[part], r_kv.at[1, yy])
        ov[part, :] = (dva[here, :] + rva[part, :]).astype(BF16)
        give(k, ov, dv_ref, 2)
        took(rka.at[part], r_kv.at[0, yy])
        ok[part, :] = (dka[here, :] + rka[part, :]).astype(BF16)
        give(k, ok, dk_ref, 1)
    for k in range(4):
        yy = group(k)
        part = rows(yy * GROUP, GROUP)
        took(dqr.at[part], r_dz.at[yy])
        oq[part, :] = (dqa[part, :] + dqr[part, :].astype(F32)).astype(BF16)
        give(k, oq, dq_ref, 0)

    sent = pl.ds(0, HALF - ROWS)
    for a in range(4):
        took(qb.at[0, sent], s_in.at[a])
    took(drec.at[pl.ds(0, CHIPS - 1)], s_d)
    for a in range(2):
        took(qb.at[0], s_z.at[a])
        took(qb.at[0], s_c.at[a])
        took(rka, s_kv.at[a])
    tell.wait_send()
    took(st_oth, s_so)
    took(dqs, s_dz)
    for a, out in enumerate((dq_ref, dk_ref, dv_ref)):
        took(out, r_out.at[a])
        took(qb.at[0, sent], s_out.at[a])


def place(dq, dk, dv, dq_out, dk_out, dv_out, sem):
    copies = [
        pltpu.make_async_copy(src, dst, sem.at[n])
        for n, (src, dst) in enumerate(((dq, dq_out), (dk, dk_out), (dv, dv_out)))
    ]
    for copy in copies:
        copy.start()
    for copy in copies:
        copy.wait()


def body(queries, keys, values, outputs, d_outputs, tile_mask, tile_order):
    half = (HALF, DH)
    dma = pltpu.SemaphoreType.DMA
    hbm = pl.BlockSpec(memory_space=pl.ANY)
    grads = pl.pallas_call(
        kernel,
        out_shape=[jax.ShapeDtypeStruct(queries.shape, BF16)] * 3,
        in_specs=[hbm] * 7,
        out_specs=[hbm] * 3,
        scratch_shapes=[
            pltpu.VMEM((2,) + half, BF16),
            pltpu.VMEM((2 * HALF, DH), BF16),
            pltpu.VMEM((2 * HALF, DH), BF16),
            pltpu.VMEM((2,) + half, BF16),
            pltpu.VMEM((2, 4, 2 * HALF, GROUP), F32),
            pltpu.VMEM((2 * HALF, DH), F32),
            pltpu.VMEM((2 * HALF, DH), F32),
            pltpu.VMEM(half, F32),
            pltpu.VMEM(half, F32),
            pltpu.VMEM(half, F32),
            pltpu.VMEM(half, BF16),
            pltpu.VMEM(half, BF16),
            pltpu.VMEM(half, BF16),
            pltpu.VMEM(half, BF16),
            pltpu.VMEM(half, BF16),
            pltpu.VMEM(outputs.shape, BF16),
            pltpu.VMEM(outputs.shape, BF16),
            pltpu.SMEM(tile_mask.shape, jnp.int32),
            pltpu.SMEM(tile_order.shape, jnp.int32),
            pltpu.VMEM((BLOCK, BLOCK), F32),
            pltpu.VMEM((CHIPS, 1, BLOCK), F32),
            pltpu.VMEM((CHIPS, 1, BLOCK), F32),
            pltpu.VMEM((4, 3, 1, GROUP), F32),
            pltpu.VMEM((4, 2, 1, GROUP), F32),
            pltpu.VMEM((4, 3, 1, GROUP), F32),
            pltpu.VMEM((4, 2, 1, GROUP), F32),
            pltpu.VMEM((2, 16, 1, HALF), F32),
            dma((4,)),
            dma((4,)), dma((4, 4)),
            dma((2,)), dma((2, 4)),
            dma((2,)), dma((2,)),
            dma, dma,
            dma, dma,
            dma, dma((4,)),
            dma, dma((4,)),
            dma((2,)), dma((2, 4)),
            dma((3,)), dma((3,)),
        ],
        compiler_params=pltpu.CompilerParams(
            collective_id=0, has_side_effects=True, vmem_limit_bytes=56 * 2**20
        ),
        cost_estimate=pl.CostEstimate(flops=5 * 2**30, bytes_accessed=2**21, transcendentals=2**22),
        name="attention_backward",
    )(queries, keys, values, outputs, d_outputs, tile_mask, tile_order)
    return pl.pallas_call(
        place,
        out_shape=[jax.ShapeDtypeStruct(queries.shape, BF16)] * 3,
        in_specs=[pl.BlockSpec(memory_space=pltpu.VMEM)] * 3,
        out_specs=[hbm] * 3,
        scratch_shapes=[dma((3,))],
        name="place",
    )(*grads)


def solution(mesh):
    split = P(("dp", "blk", "head"), None)
    return jax.shard_map(
        body,
        mesh=mesh,
        in_specs=(split,) * 5 + (P(), P()),
        out_specs=(split,) * 3,
        check_vma=False,
    )
```

```python
import jax
import jax.numpy as jnp
from jax import lax
from jax.experimental import pallas as pl
from jax.experimental.pallas import tpu as pltpu
from jax.sharding import PartitionSpec as P

DH = 128
BLOCK = 128
ROWS = 64
CHIPS = 16
GROUP = 4 * ROWS
HALF = CHIPS * ROWS
SCALE = DH**-0.5
LOG2E = 1.4426950408889634
MESH = pl.DeviceIdType.MESH
BF16 = jnp.bfloat16
F32 = jnp.float32

NT = (((1,), (1,)), ((), ()))
NN = (((1,), (0,)), ((), ()))
TN = (((0,), (0,)), ((), ()))


def mm(a, b, dims):
    return lax.dot_general(a, b, dims, preferred_element_type=F32)


def rows(start, size):
    return pl.ds(pl.multiple_of(start, size), size)


def kernel(
    q_ref, k_ref, v_ref, o_ref, g_ref, mask_hbm, order_hbm,
    dq_ref, dk_ref, dv_ref,
    qb, kb, vb, gb, ee, dka, dva, rka, rva, dqa, dqs, dqr, oq, ok, ov,
    ol, gl, mask_ref, order_ref, dcol, dsrc, drec, st_own, st_oth, pr_own, pr_oth, bias,
    s_ld, s_in, r_in, s_z, r_z, s_c, r_c, s_d, r_d, s_st, r_st, s_so, r_so, s_dz, r_dz, s_kv, r_kv, s_out, r_out,
):
    blk = lax.axis_index("blk")
    hd = lax.axis_index("head")
    dp = lax.axis_index("dp")
    y, c = blk // 2, blk % 2
    g, x = hd // 4, hd % 4
    me = y * 4 + x

    def plane(px, py):
        return (py * 2 + c, g * 4 + px, dp)

    across = (blk, (1 - g) * 4 + x, dp)
    sibling = (y * 2 + 1 - c, hd, dp)

    def remote(src, dst, ss, rs, to):
        return pltpu.make_async_remote_copy(
            src_ref=src, dst_ref=dst, send_sem=ss, recv_sem=rs, device_id=to, device_id_type=MESH
        )

    def took(ref, sem):
        pltpu.make_async_copy(ref, ref, sem).wait()

    def peer(k):
        px, py = (x + k % 4) % 4, (y + k // 4) % 4
        return px, py, py * 4 + px

    barrier = pltpu.get_barrier_semaphore()

    def greet(k, carry):
        px, py, unused = peer(k)
        pl.semaphore_signal(barrier, inc=1, device_id=plane(px, py), device_id_type=MESH)
        return carry

    pl.semaphore_signal(barrier, inc=1, device_id=across, device_id_type=MESH)
    lax.fori_loop(1, CHIPS, greet, 0)
    pl.semaphore_signal(barrier, inc=1, device_id=sibling, device_id_type=MESH)

    loads = [
        pltpu.make_async_copy(src, dst, s_ld.at[n])
        for n, (src, dst) in enumerate(((o_ref, ol), (g_ref, gl), (mask_hbm, mask_ref), (order_hbm, order_ref)))
    ]
    for load in loads:
        load.start()
    pl.semaphore_wait(barrier, 17)

    sources = (q_ref, k_ref, g_ref, v_ref)
    mine = rows(me * ROWS, ROWS)
    mine_kv = rows(c * HALF + me * ROWS, ROWS)
    targets = (qb.at[0, mine], kb.at[mine_kv], gb.at[0, mine], vb.at[mine_kv])
    for a in range(4):
        here = sources[a].at[:, rows(me * DH, DH)]
        pltpu.make_async_copy(here, targets[a], r_in.at[a, y]).start()

        def send(k, carry):
            px, py, who = peer(k)
            remote(
                sources[a].at[:, rows(who * DH, DH)], targets[a], s_in.at[a], r_in.at[a, y], plane(px, py)
            ).start()
            return carry

        lax.fori_loop(1, CHIPS, send, 0)

    def group(k):
        return (y + 4 - k) % 4

    def forward_z(a, buf, first, last):
        def one(k, carry):
            yy = group((k + a) % 4)
            part = rows(yy * GROUP, GROUP)
            took(buf.at[0, part], r_in.at[2 * a, yy])
            remote(buf.at[0, part], buf.at[1, part], s_z.at[a], r_z.at[a, yy], across).start()
            return carry

        lax.fori_loop(first, last, one, 0)

    def forward_core(a, buf):
        def one(k, carry):
            yy = group(k)
            part = rows(c * HALF + yy * GROUP, GROUP)
            took(buf.at[part], r_in.at[2 * a + 1, yy])
            remote(buf.at[part], buf.at[part], s_c.at[a], r_c.at[a], sibling).start()
            return carry

        lax.fori_loop(0, 4, one, 0)

    forward_z(0, qb, 0, 4)

    for load in loads:
        load.wait()

    dcol[...] = jnp.zeros_like(dcol)
    prod = gl[...].astype(F32) * ol[...].astype(F32)
    lane = lax.broadcasted_iota(jnp.int32, (ROWS, BLOCK), 1)
    cols = jnp.zeros((ROWS, BLOCK), F32)
    for h in range(CHIPS):
        part = jnp.sum(prod[:, h * DH : (h + 1) * DH], axis=1, keepdims=True)
        cols = jnp.where(lane == h, part, cols)
    dcol[rows((x % 2) * ROWS, ROWS), :] = cols
    turned = dcol[...].T
    for h in range(CHIPS):
        dsrc[h] = turned[h : h + 1, :]

    pltpu.make_async_copy(dsrc.at[me], drec.at[me], r_d).start()

    def send_delta(k, carry):
        px, py, who = peer(k)
        remote(dsrc.at[who], drec.at[me], s_d, r_d, plane(px, py)).start()
        return carry

    lax.fori_loop(1, CHIPS, send_delta, 0)

    def block_of(j, core, half):
        return ((j // 2) * 2 + core) * 4 + half * 2 + j % 2

    def bias_row(i, carry):
        key_tile = order_ref[block_of(i % 8, i // 8, g)]
        for half in range(2):
            for j in range(8):
                query_tile = order_ref[block_of(j, c, g if half == 0 else 1 - g)]
                allowed = mask_ref[query_tile, key_tile]
                value = jnp.where(allowed == 1, 0.0, -1.0e30).astype(F32)
                bias[half, i, :, j * BLOCK : (j + 1) * BLOCK] = jnp.full((1, BLOCK), value, F32)
        return carry

    lax.fori_loop(0, 16, bias_row, 0)
    dka[...] = jnp.zeros_like(dka)
    dva[...] = jnp.zeros_like(dva)

    def weigh(half, yy, stats):
        lanes = rows(yy * GROUP, GROUP)
        s = mm(kb[...], qb[half, lanes, :], NT) * (SCALE * LOG2E)
        top = jnp.full((8, GROUP), -3.0e38, F32)
        for i in range(16):
            part = s[i * BLOCK : (i + 1) * BLOCK] + bias[half, i, :, lanes]
            ee[half, yy, i * BLOCK : (i + 1) * BLOCK, :] = part
            top = jnp.maximum(top, jnp.max(part.reshape(BLOCK // 8, 8, GROUP), axis=0))
        top = jnp.max(top, axis=0, keepdims=True)
        e = jnp.exp2(ee[half, yy] - top)
        ee[half, yy] = e
        total = jnp.sum(e.reshape(2 * HALF // 8, 8, GROUP), axis=0)
        stats[yy, 0] = top
        stats[yy, 1] = jnp.sum(total, axis=0, keepdims=True)

    def gradients(half, yy, stats, theirs, delta):
        lanes = rows(yy * GROUP, GROUP)
        query = qb[half, lanes, :]
        dout = gb[half, lanes, :]
        top, total, top_r, total_r = stats[yy, 0], stats[yy, 1], theirs[yy, 0], theirs[yy, 1]
        high = jnp.maximum(top, top_r)
        ours = jnp.exp2(top - high)
        factor = ours / (total * ours + total_r * jnp.exp2(top_r - high))
        e = ee[half, yy]
        ds = (e * (factor * SCALE) * (mm(vb[...], dout, NT) - delta)).astype(BF16)
        dva[...] += mm((e * factor).astype(BF16), dout, NN)
        dka[...] += mm(ds, query, NN)
        return mm(ds, kb[...], TN)

    def weigh_own(k, carry):
        weigh(0, group(k), st_own)
        return carry

    def weigh_other(k, carry):
        yy = group(k)
        took(qb.at[1, rows(yy * GROUP, GROUP)], r_z.at[0, yy])
        weigh(1, yy, st_oth)
        remote(st_oth.at[yy], pr_oth.at[yy], s_so, r_so.at[yy], across).start()
        return carry

    def own(k, carry):
        yy = group(k)
        took(pr_oth.at[yy], r_so.at[yy])
        dqa[rows(yy * GROUP, GROUP), :] = gradients(0, yy, st_own, pr_oth, st_own[yy, 2])
        return carry

    def other(k, carry):
        yy = group((k + 1) % 4)
        part = rows(yy * GROUP, GROUP)
        took(gb.at[1, part], r_z.at[1, yy])
        dqs[part, :] = gradients(1, yy, st_oth, pr_own, pr_own[yy, 2]).astype(BF16)
        remote(dqs.at[part], dqr.at[part], s_dz, r_dz.at[yy], across).start()
        return carry

    forward_core(0, kb)
    took(kb.at[pl.ds((1 - c) * HALF, HALF)], r_c.at[0])
    lax.fori_loop(0, 4, weigh_own, 0)
    took(drec, r_d)
    for j in range(8):
        st_own[j // 2, 2, :, j % 2 * BLOCK : (j % 2 + 1) * BLOCK] = drec[2 * j] + drec[2 * j + 1]
    tell = remote(st_own, pr_own, s_st, r_st, across)
    tell.start()
    forward_z(1, gb, 0, 1)
    lax.fori_loop(0, 3, weigh_other, 0)
    forward_z(1, gb, 1, 3)
    forward_core(1, vb)
    lax.fori_loop(3, 4, weigh_other, 0)
    forward_z(1, gb, 3, 4)
    took(vb.at[pl.ds((1 - c) * HALF, HALF)], r_c.at[1])
    lax.fori_loop(0, 3, own, 0)
    tell.wait_recv()
    lax.fori_loop(0, 2, other, 0)
    lax.fori_loop(3, 4, own, 0)
    lax.fori_loop(2, 4, other, 0)

    for k in (1, 2, 3, 0):
        yy = group(k)
        part = rows(yy * GROUP, GROUP)
        there = rows((1 - c) * HALF + yy * GROUP, GROUP)
        remote(dva.at[there], rva.at[part], s_kv.at[1], r_kv.at[1, yy], sibling).start()
        remote(dka.at[there], rka.at[part], s_kv.at[0], r_kv.at[0, yy], sibling).start()

    def give(k, buf, out, a):
        yy = group(k)
        for kx in (2, 1, 3, 0):
            px = (x + kx) % 4
            piece = buf.at[rows((yy * 4 + px) * ROWS, ROWS)]
            home = out.at[:, rows(me * DH, DH)]
            if k == 0 and kx == 0:
                pltpu.make_async_copy(piece, home, r_out.at[a]).start()
            else:
                remote(piece, home, s_out.at[a], r_out.at[a], plane(px, yy)).start()

    for k in (1, 2, 3, 0):
        yy = group(k)
        part = rows(yy * GROUP, GROUP)
        here = rows(c * HALF + yy * GROUP, GROUP)
        took(rva.at[part], r_kv.at[1, yy])
        ov[part, :] = (dva[here, :] + rva[part, :]).astype(BF16)
        give(k, ov, dv_ref, 2)
        took(rka.at[part], r_kv.at[0, yy])
        ok[part, :] = (dka[here, :] + rka[part, :]).astype(BF16)
        give(k, ok, dk_ref, 1)
    for k in (1, 2, 3, 0):
        yy = group(k)
        part = rows(yy * GROUP, GROUP)
        took(dqr.at[part], r_dz.at[yy])
        oq[part, :] = (dqa[part, :] + dqr[part, :].astype(F32)).astype(BF16)
        give(k, oq, dq_ref, 0)

    sent = pl.ds(0, HALF - ROWS)
    for a in range(4):
        took(qb.at[0, sent], s_in.at[a])
    took(drec.at[pl.ds(0, CHIPS - 1)], s_d)
    for a in range(2):
        took(qb.at[0], s_z.at[a])
        took(qb.at[0], s_c.at[a])
        took(rka, s_kv.at[a])
    tell.wait_send()
    took(st_oth, s_so)
    took(dqs, s_dz)
    for a, out in enumerate((dq_ref, dk_ref, dv_ref)):
        took(out, r_out.at[a])
        took(qb.at[0, sent], s_out.at[a])


def place(dq, dk, dv, dq_out, dk_out, dv_out, sem):
    copies = [
        pltpu.make_async_copy(src, dst, sem.at[n])
        for n, (src, dst) in enumerate(((dq, dq_out), (dk, dk_out), (dv, dv_out)))
    ]
    for copy in copies:
        copy.start()
    for copy in copies:
        copy.wait()


def body(queries, keys, values, outputs, d_outputs, tile_mask, tile_order):
    half = (HALF, DH)
    dma = pltpu.SemaphoreType.DMA
    hbm = pl.BlockSpec(memory_space=pl.ANY)
    grads = pl.pallas_call(
        kernel,
        out_shape=[jax.ShapeDtypeStruct(queries.shape, BF16)] * 3,
        in_specs=[hbm] * 7,
        out_specs=[hbm] * 3,
        scratch_shapes=[
            pltpu.VMEM((2,) + half, BF16),
            pltpu.VMEM((2 * HALF, DH), BF16),
            pltpu.VMEM((2 * HALF, DH), BF16),
            pltpu.VMEM((2,) + half, BF16),
            pltpu.VMEM((2, 4, 2 * HALF, GROUP), F32),
            pltpu.VMEM((2 * HALF, DH), F32),
            pltpu.VMEM((2 * HALF, DH), F32),
            pltpu.VMEM(half, F32),
            pltpu.VMEM(half, F32),
            pltpu.VMEM(half, F32),
            pltpu.VMEM(half, BF16),
            pltpu.VMEM(half, BF16),
            pltpu.VMEM(half, BF16),
            pltpu.VMEM(half, BF16),
            pltpu.VMEM(half, BF16),
            pltpu.VMEM(outputs.shape, BF16),
            pltpu.VMEM(outputs.shape, BF16),
            pltpu.SMEM(tile_mask.shape, jnp.int32),
            pltpu.SMEM(tile_order.shape, jnp.int32),
            pltpu.VMEM((BLOCK, BLOCK), F32),
            pltpu.VMEM((CHIPS, 1, BLOCK), F32),
            pltpu.VMEM((CHIPS, 1, BLOCK), F32),
            pltpu.VMEM((4, 3, 1, GROUP), F32),
            pltpu.VMEM((4, 2, 1, GROUP), F32),
            pltpu.VMEM((4, 3, 1, GROUP), F32),
            pltpu.VMEM((4, 2, 1, GROUP), F32),
            pltpu.VMEM((2, 16, 1, HALF), F32),
            dma((4,)),
            dma((4,)), dma((4, 4)),
            dma((2,)), dma((2, 4)),
            dma((2,)), dma((2,)),
            dma, dma,
            dma, dma,
            dma, dma((4,)),
            dma, dma((4,)),
            dma((2,)), dma((2, 4)),
            dma((3,)), dma((3,)),
        ],
        compiler_params=pltpu.CompilerParams(
            collective_id=0, has_side_effects=True, vmem_limit_bytes=56 * 2**20
        ),
        cost_estimate=pl.CostEstimate(flops=5 * 2**30, bytes_accessed=2**21, transcendentals=2**22),
        name="attention_backward",
    )(queries, keys, values, outputs, d_outputs, tile_mask, tile_order)
    return pl.pallas_call(
        place,
        out_shape=[jax.ShapeDtypeStruct(queries.shape, BF16)] * 3,
        in_specs=[pl.BlockSpec(memory_space=pltpu.VMEM)] * 3,
        out_specs=[hbm] * 3,
        scratch_shapes=[dma((3,))],
        name="place",
    )(*grads)


def solution(mesh):
    split = P(("dp", "blk", "head"), None)
    return jax.shard_map(
        body,
        mesh=mesh,
        in_specs=(split,) * 5 + (P(), P()),
        out_specs=(split,) * 3,
        check_vma=False,
    )
```

```python
import jax
import jax.numpy as jnp
from jax import lax
from jax.experimental import pallas as pl
from jax.experimental.pallas import tpu as pltpu
from jax.sharding import PartitionSpec as P

DH = 128
BLOCK = 128
ROWS = 64
CHIPS = 16
GROUP = 4 * ROWS
HALF = CHIPS * ROWS
SCALE = DH**-0.5
LOG2E = 1.4426950408889634
MESH = pl.DeviceIdType.MESH
BF16 = jnp.bfloat16
F32 = jnp.float32

NT = (((1,), (1,)), ((), ()))
NN = (((1,), (0,)), ((), ()))
TN = (((0,), (0,)), ((), ()))


def mm(a, b, dims):
    return lax.dot_general(a, b, dims, preferred_element_type=F32)


def rows(start, size):
    return pl.ds(pl.multiple_of(start, size), size)


def kernel(
    q_ref, k_ref, v_ref, o_ref, g_ref, mask_hbm, order_hbm,
    dq_ref, dk_ref, dv_ref,
    qb, kb, vb, gb, ee, dka, dva, rka, rva, dqa, dqs, dqr, oq, ok, ov,
    ol, gl, mask_ref, order_ref, dcol, dsrc, drec, st_own, st_oth, pr_own, pr_oth, bias,
    s_ld, s_in, r_in, s_z, r_z, s_c, r_c, s_d, r_d, s_st, r_st, s_so, r_so, s_dz, r_dz, s_kv, r_kv, s_out, r_out,
):
    blk = lax.axis_index("blk")
    hd = lax.axis_index("head")
    dp = lax.axis_index("dp")
    y, c = blk // 2, blk % 2
    g, x = hd // 4, hd % 4
    me = y * 4 + x

    def plane(px, py):
        return (py * 2 + c, g * 4 + px, dp)

    across = (blk, (1 - g) * 4 + x, dp)
    sibling = (y * 2 + 1 - c, hd, dp)

    def remote(src, dst, ss, rs, to):
        return pltpu.make_async_remote_copy(
            src_ref=src, dst_ref=dst, send_sem=ss, recv_sem=rs, device_id=to, device_id_type=MESH
        )

    def took(ref, sem):
        pltpu.make_async_copy(ref, ref, sem).wait()

    def peer(k):
        px, py = (x + k % 4) % 4, (y + k // 4) % 4
        return px, py, py * 4 + px

    barrier = pltpu.get_barrier_semaphore()

    def greet(k, carry):
        px, py, unused = peer(k)
        pl.semaphore_signal(barrier, inc=1, device_id=plane(px, py), device_id_type=MESH)
        return carry

    pl.semaphore_signal(barrier, inc=1, device_id=across, device_id_type=MESH)
    lax.fori_loop(1, CHIPS, greet, 0)
    pl.semaphore_signal(barrier, inc=1, device_id=sibling, device_id_type=MESH)

    loads = [
        pltpu.make_async_copy(src, dst, s_ld.at[n])
        for n, (src, dst) in enumerate(((o_ref, ol), (g_ref, gl), (mask_hbm, mask_ref), (order_hbm, order_ref)))
    ]
    for load in loads:
        load.start()
    pl.semaphore_wait(barrier, 17)

    sources = (q_ref, k_ref, g_ref, v_ref)
    mine = rows(me * ROWS, ROWS)
    mine_kv = rows(c * HALF + me * ROWS, ROWS)
    targets = (qb.at[0, mine], kb.at[mine_kv], gb.at[0, mine], vb.at[mine_kv])
    for a in range(4):
        here = sources[a].at[:, rows(me * DH, DH)]
        pltpu.make_async_copy(here, targets[a], r_in.at[a, y]).start()

        def send(k, carry):
            px, py, who = peer(k)
            remote(
                sources[a].at[:, rows(who * DH, DH)], targets[a], s_in.at[a], r_in.at[a, y], plane(px, py)
            ).start()
            return carry

        lax.fori_loop(1, CHIPS, send, 0)

    def group(k):
        return (y + 4 - k) % 4

    def forward_z(a, buf, first, last):
        def one(k, carry):
            yy = group((k + a) % 4)
            part = rows(yy * GROUP, GROUP)
            took(buf.at[0, part], r_in.at[2 * a, yy])
            remote(buf.at[0, part], buf.at[1, part], s_z.at[a], r_z.at[a, yy], across).start()
            return carry

        lax.fori_loop(first, last, one, 0)

    def forward_core(a, buf):
        def one(k, carry):
            yy = group(k)
            part = rows(c * HALF + yy * GROUP, GROUP)
            took(buf.at[part], r_in.at[2 * a + 1, yy])
            remote(buf.at[part], buf.at[part], s_c.at[a], r_c.at[a], sibling).start()
            return carry

        lax.fori_loop(0, 4, one, 0)

    forward_z(0, qb, 0, 4)

    for load in loads:
        load.wait()

    dcol[...] = jnp.zeros_like(dcol)
    prod = gl[...].astype(F32) * ol[...].astype(F32)
    lane = lax.broadcasted_iota(jnp.int32, (ROWS, BLOCK), 1)
    cols = jnp.zeros((ROWS, BLOCK), F32)
    for h in range(CHIPS):
        part = jnp.sum(prod[:, h * DH : (h + 1) * DH], axis=1, keepdims=True)
        cols = jnp.where(lane == h, part, cols)
    dcol[rows((x % 2) * ROWS, ROWS), :] = cols
    turned = dcol[...].T
    for h in range(CHIPS):
        dsrc[h] = turned[h : h + 1, :]

    pltpu.make_async_copy(dsrc.at[me], drec.at[me], r_d).start()

    def send_delta(k, carry):
        px, py, who = peer(k)
        remote(dsrc.at[who], drec.at[me], s_d, r_d, plane(px, py)).start()
        return carry

    lax.fori_loop(1, CHIPS, send_delta, 0)

    def block_of(j, core, half):
        return ((j // 2) * 2 + core) * 4 + half * 2 + j % 2

    def bias_row(i, carry):
        key_tile = order_ref[block_of(i % 8, i // 8, g)]
        for half in range(2):
            for j in range(8):
                query_tile = order_ref[block_of(j, c, g if half == 0 else 1 - g)]
                allowed = mask_ref[query_tile, key_tile]
                value = jnp.where(allowed == 1, 0.0, -1.0e30).astype(F32)
                bias[half, i, :, j * BLOCK : (j + 1) * BLOCK] = jnp.full((1, BLOCK), value, F32)
        return carry

    lax.fori_loop(0, 16, bias_row, 0)
    dka[...] = jnp.zeros_like(dka)
    dva[...] = jnp.zeros_like(dva)

    def weigh(half, yy, stats):
        lanes = rows(yy * GROUP, GROUP)
        s = mm(kb[...], qb[half, lanes, :], NT) * (SCALE * LOG2E)
        top = jnp.full((8, GROUP), -3.0e38, F32)
        for i in range(16):
            part = s[i * BLOCK : (i + 1) * BLOCK] + bias[half, i, :, lanes]
            ee[half, yy, i * BLOCK : (i + 1) * BLOCK, :] = part
            top = jnp.maximum(top, jnp.max(part.reshape(BLOCK // 8, 8, GROUP), axis=0))
        top = jnp.max(top, axis=0, keepdims=True)
        e = jnp.exp2(ee[half, yy] - top)
        ee[half, yy] = e
        total = jnp.sum(e.reshape(2 * HALF // 8, 8, GROUP), axis=0)
        stats[yy, 0] = top
        stats[yy, 1] = jnp.sum(total, axis=0, keepdims=True)

    def gradients(half, yy, stats, theirs, delta, keys=slice(None)):
        lanes = rows(yy * GROUP, GROUP)
        query = qb[half, lanes, :]
        dout = gb[half, lanes, :]
        top, total, top_r, total_r = stats[yy, 0], stats[yy, 1], theirs[yy, 0], theirs[yy, 1]
        high = jnp.maximum(top, top_r)
        ours = jnp.exp2(top - high)
        factor = ours / (total * ours + total_r * jnp.exp2(top_r - high))
        e = ee[half, yy, keys, :]
        ds = (e * (factor * SCALE) * (mm(vb[keys, :], dout, NT) - delta)).astype(BF16)
        dva[keys, :] += mm((e * factor).astype(BF16), dout, NN)
        dka[keys, :] += mm(ds, query, NN)
        return mm(ds, kb[keys, :], TN)

    def weigh_own(k, carry):
        weigh(0, group(k), st_own)
        return carry

    def weigh_other(k, carry):
        yy = group(k)
        took(qb.at[1, rows(yy * GROUP, GROUP)], r_z.at[0, yy])
        weigh(1, yy, st_oth)
        remote(st_oth.at[yy], pr_oth.at[yy], s_so, r_so.at[yy], across).start()
        return carry

    def own(k, carry):
        yy = group(k)
        took(pr_oth.at[yy], r_so.at[yy])
        dqa[rows(yy * GROUP, GROUP), :] = gradients(0, yy, st_own, pr_oth, st_own[yy, 2])
        return carry

    def other(k, carry):
        yy = group((k + 1) % 4)
        part = rows(yy * GROUP, GROUP)
        took(gb.at[1, part], r_z.at[1, yy])
        dqs[part, :] = gradients(1, yy, st_oth, pr_own, pr_own[yy, 2]).astype(BF16)
        remote(dqs.at[part], dqr.at[part], s_dz, r_dz.at[yy], across).start()
        return carry

    forward_core(0, kb)
    took(kb.at[pl.ds((1 - c) * HALF, HALF)], r_c.at[0])
    lax.fori_loop(0, 4, weigh_own, 0)
    took(drec, r_d)
    for j in range(8):
        st_own[j // 2, 2, :, j % 2 * BLOCK : (j % 2 + 1) * BLOCK] = drec[2 * j] + drec[2 * j + 1]
    tell = remote(st_own, pr_own, s_st, r_st, across)
    tell.start()
    forward_z(1, gb, 0, 1)
    lax.fori_loop(0, 3, weigh_other, 0)
    forward_z(1, gb, 1, 3)
    forward_core(1, vb)
    lax.fori_loop(3, 4, weigh_other, 0)
    forward_z(1, gb, 3, 4)
    took(vb.at[pl.ds((1 - c) * HALF, HALF)], r_c.at[1])
    lax.fori_loop(0, 3, own, 0)
    tell.wait_recv()
    lax.fori_loop(0, 2, other, 0)
    lax.fori_loop(3, 4, own, 0)
    lax.fori_loop(2, 3, other, 0)

    last = group(0)
    part_last = rows(last * GROUP, GROUP)
    took(gb.at[1, part_last], r_z.at[1, last])
    theirs = rows((1 - c) * HALF, HALF)
    dq_last = gradients(1, last, st_oth, pr_own, pr_own[last, 2], theirs)
    for k in (1, 2, 3, 0):
        yy = group(k)
        part = rows(yy * GROUP, GROUP)
        there = rows((1 - c) * HALF + yy * GROUP, GROUP)
        remote(dva.at[there], rva.at[part], s_kv.at[1], r_kv.at[1, yy], sibling).start()
        remote(dka.at[there], rka.at[part], s_kv.at[0], r_kv.at[0, yy], sibling).start()
    dq_last += gradients(1, last, st_oth, pr_own, pr_own[last, 2], rows(c * HALF, HALF))
    dqs[part_last, :] = dq_last.astype(BF16)
    remote(dqs.at[part_last], dqr.at[part_last], s_dz, r_dz.at[last], across).start()


    def give(k, buf, out, a):
        yy = group(k)
        for kx in (2, 1, 3, 0):
            px = (x + kx) % 4
            piece = buf.at[rows((yy * 4 + px) * ROWS, ROWS)]
            home = out.at[:, rows(me * DH, DH)]
            if k == 0 and kx == 0:
                pltpu.make_async_copy(piece, home, r_out.at[a]).start()
            else:
                remote(piece, home, s_out.at[a], r_out.at[a], plane(px, yy)).start()

    for k in (1, 2, 3, 0):
        yy = group(k)
        part = rows(yy * GROUP, GROUP)
        here = rows(c * HALF + yy * GROUP, GROUP)
        took(rva.at[part], r_kv.at[1, yy])
        ov[part, :] = (dva[here, :] + rva[part, :]).astype(BF16)
        give(k, ov, dv_ref, 2)
        took(rka.at[part], r_kv.at[0, yy])
        ok[part, :] = (dka[here, :] + rka[part, :]).astype(BF16)
        give(k, ok, dk_ref, 1)
    for k in (1, 2, 3, 0):
        yy = group(k)
        part = rows(yy * GROUP, GROUP)
        took(dqr.at[part], r_dz.at[yy])
        oq[part, :] = (dqa[part, :] + dqr[part, :].astype(F32)).astype(BF16)
        give(k, oq, dq_ref, 0)

    sent = pl.ds(0, HALF - ROWS)
    for a in range(4):
        took(qb.at[0, sent], s_in.at[a])
    took(drec.at[pl.ds(0, CHIPS - 1)], s_d)
    for a in range(2):
        took(qb.at[0], s_z.at[a])
        took(qb.at[0], s_c.at[a])
        took(rka, s_kv.at[a])
    tell.wait_send()
    took(st_oth, s_so)
    took(dqs, s_dz)
    for a, out in enumerate((dq_ref, dk_ref, dv_ref)):
        took(out, r_out.at[a])
        took(qb.at[0, sent], s_out.at[a])


def place(dq, dk, dv, dq_out, dk_out, dv_out, sem):
    copies = [
        pltpu.make_async_copy(src, dst, sem.at[n])
        for n, (src, dst) in enumerate(((dq, dq_out), (dk, dk_out), (dv, dv_out)))
    ]
    for copy in copies:
        copy.start()
    for copy in copies:
        copy.wait()


def body(queries, keys, values, outputs, d_outputs, tile_mask, tile_order):
    half = (HALF, DH)
    dma = pltpu.SemaphoreType.DMA
    hbm = pl.BlockSpec(memory_space=pl.ANY)
    grads = pl.pallas_call(
        kernel,
        out_shape=[jax.ShapeDtypeStruct(queries.shape, BF16)] * 3,
        in_specs=[hbm] * 7,
        out_specs=[hbm] * 3,
        scratch_shapes=[
            pltpu.VMEM((2,) + half, BF16),
            pltpu.VMEM((2 * HALF, DH), BF16),
            pltpu.VMEM((2 * HALF, DH), BF16),
            pltpu.VMEM((2,) + half, BF16),
            pltpu.VMEM((2, 4, 2 * HALF, GROUP), F32),
            pltpu.VMEM((2 * HALF, DH), F32),
            pltpu.VMEM((2 * HALF, DH), F32),
            pltpu.VMEM(half, F32),
            pltpu.VMEM(half, F32),
            pltpu.VMEM(half, F32),
            pltpu.VMEM(half, BF16),
            pltpu.VMEM(half, BF16),
            pltpu.VMEM(half, BF16),
            pltpu.VMEM(half, BF16),
            pltpu.VMEM(half, BF16),
            pltpu.VMEM(outputs.shape, BF16),
            pltpu.VMEM(outputs.shape, BF16),
            pltpu.SMEM(tile_mask.shape, jnp.int32),
            pltpu.SMEM(tile_order.shape, jnp.int32),
            pltpu.VMEM((BLOCK, BLOCK), F32),
            pltpu.VMEM((CHIPS, 1, BLOCK), F32),
            pltpu.VMEM((CHIPS, 1, BLOCK), F32),
            pltpu.VMEM((4, 3, 1, GROUP), F32),
            pltpu.VMEM((4, 2, 1, GROUP), F32),
            pltpu.VMEM((4, 3, 1, GROUP), F32),
            pltpu.VMEM((4, 2, 1, GROUP), F32),
            pltpu.VMEM((2, 16, 1, HALF), F32),
            dma((4,)),
            dma((4,)), dma((4, 4)),
            dma((2,)), dma((2, 4)),
            dma((2,)), dma((2,)),
            dma, dma,
            dma, dma,
            dma, dma((4,)),
            dma, dma((4,)),
            dma((2,)), dma((2, 4)),
            dma((3,)), dma((3,)),
        ],
        compiler_params=pltpu.CompilerParams(
            collective_id=0, has_side_effects=True, vmem_limit_bytes=56 * 2**20
        ),
        cost_estimate=pl.CostEstimate(flops=5 * 2**30, bytes_accessed=2**21, transcendentals=2**22),
        name="attention_backward",
    )(queries, keys, values, outputs, d_outputs, tile_mask, tile_order)
    return pl.pallas_call(
        place,
        out_shape=[jax.ShapeDtypeStruct(queries.shape, BF16)] * 3,
        in_specs=[pl.BlockSpec(memory_space=pltpu.VMEM)] * 3,
        out_specs=[hbm] * 3,
        scratch_shapes=[dma((3,))],
        name="place",
    )(*grads)


def solution(mesh):
    split = P(("dp", "blk", "head"), None)
    return jax.shard_map(
        body,
        mesh=mesh,
        in_specs=(split,) * 5 + (P(), P()),
        out_specs=(split,) * 3,
        check_vma=False,
    )
```
